256 devices in a mesh: kp: 64 (over z, y, core), eig: 4 (over x).
Axes of the slice: x: 4, y: 4, z: 8, core: 2. Of those that a mesh axis runs over, the one named last changes fastest.
Arguments:
- cond_dens: bfloat16 [64, 64, 64, 2048], P(None, 'kp', None, 'eig'), may hold values from -0.75 to 0.75
- val_dens: bfloat16 [64, 64, 64, 2048], P('kp', None, None, 'eig'), may hold values from -0.75 to 0.75
- trial_vecs: bfloat16 [32, 64, 512], replicated, may hold values from -6 to 6
- eig_vals: float32 [2048], P('eig'), may hold values from 0.005 to 0.05
- block_pairs: int32 [64, 2], replicated, may hold values from 0 to 31, as said below
- slot_block: int32 [64], replicated, may hold values from 0 to 63, each once
Outputs:
- kernel_image: float32 [2048, 512], P('kp', 'eig')
The draws below stay inside these ranges and needn't reach their ends.
Inputs may be any that keep to these rules, and one draw needn't show every extreme that they name: `block_pairs`: distinct pairs with k <= k2.
All inputs are finite; a program needn't handle non-finite values.
Results may differ from the reference program's by a relative error of at most 0.0065.
Values may be sent and summed in bfloat16 or wider, within the bound.
No kernel may reach another device: no remote copies, remote signals or barrier semaphores. Data moves between devices by JAX's collectives and lax.ppermute only.
A program may use at most 128 MiB of HBM per device.

```python
import math
import jax
import jax.numpy as jnp
import numpy as np
from jax import lax

NK = 32
NV = 64
NC = 64
NMU = 2048
NVEC = 8
NBLK = 64


def draw_block_pairs(key, part):
    key = jax.random.fold_in(key, 7)
    first, second = np.triu_indices(NK)
    order = jax.random.permutation(key, first.shape[0])[:NBLK]
    lower = jnp.asarray(first, jnp.int32)[order]
    upper = jnp.asarray(second, jnp.int32)[order]
    return jnp.stack([lower, upper], axis=1)


def levels(own_key, dims, pieces, low, largest):
    def one(axis_at, blocks):
        steps = jax.random.uniform(jax.random.fold_in(jax.random.fold_in(own_key, 6), axis_at), (blocks,), jnp.float32, low / len(pieces), largest / len(pieces))
        return jnp.repeat(jnp.exp(steps), dims[axis_at] // blocks).reshape((-1,) + (1,) * (len(dims) - axis_at - 1))

    gain = one(*pieces[0])
    for cut in pieces[1:]:
        gain = gain * one(*cut)
    return gain


def gaussian(stream_key, shape, scale, bound, cuts=(), kind=jnp.bfloat16):
    entries = jax.random.normal(stream_key, shape, jnp.float32) * scale
    if len(cuts) > 0:
        entries = levels(stream_key, shape, cuts, -0.22, 0.18) * entries
    return jnp.clip(entries, min=-bound, max=bound).astype(kind)


def setup_inputs(seed: int = 0) -> dict:
    key_of = jax.random.split(jax.random.key(seed), 7)
    cond_dens = gaussian(key_of[0], (NBLK, NC, NC, NMU), NC ** -0.5, 0.75, ((1, 64), (3, 4)))
    val_dens = gaussian(key_of[1], (NBLK, NV, NV, NMU), NV ** -0.5, 0.75, ((0, 64), (3, 4)))
    trial_vecs = gaussian(key_of[2], (NK, NV, NC * NVEC), 1.0, 6.0)
    eig_vals = jnp.clip(jnp.exp(math.log(0.05) - 2.3025851 * jax.random.uniform(key_of[3], (NMU,), jnp.float32) ** levels(key_of[3], (NMU,), ((0, 4),), -0.2, 0.2)), 0.005, 0.05)
    block_pairs = draw_block_pairs(jax.random.fold_in(key_of[6], 71), 0)
    slot_block = jax.random.permutation(key_of[5], NBLK).astype(jnp.int32)
    return dict(cond_dens=cond_dens, val_dens=val_dens, trial_vecs=trial_vecs, eig_vals=eig_vals, block_pairs=block_pairs, slot_block=slot_block)


def block_terms(cond, valence, near, far, scale):
    total_mu = cond.shape[2]
    stride_mu = min(128, total_mu)
    count = total_mu // stride_mu
    nv_bands = valence.shape[0]
    nc_bands = cond.shape[0]
    nvec = far.shape[2]

    def advance(carry, number):
        start = number * stride_mu
        cond_part = lax.dynamic_slice_in_dim(cond, start, stride_mu, 2).astype(jnp.float32)
        val_part = lax.dynamic_slice_in_dim(valence, start, stride_mu, 2).astype(jnp.float32)
        scale_part = lax.dynamic_slice_in_dim(scale, start, stride_mu, 0)
        ahead = jnp.einsum("cdm,wdn->mcwn", cond_part, far.astype(jnp.float32))
        ahead = (ahead * scale_part[:, None, None, None]).astype(jnp.bfloat16).astype(jnp.float32)
        forward = carry[0] + jnp.einsum("vwm,mcwn->vcn", val_part, ahead)
        back = jnp.einsum("cdm,vcn->mdvn", cond_part, near.astype(jnp.float32))
        back = (back * scale_part[:, None, None, None]).astype(jnp.bfloat16).astype(jnp.float32)
        mirror = carry[1] + jnp.einsum("vwm,mdvn->wdn", val_part, back)
        return (forward, mirror), None

    start_state = (jnp.zeros((nv_bands, nc_bands, nvec), jnp.float32), jnp.zeros((nv_bands, nc_bands, nvec), jnp.float32))
    result, unused = lax.scan(advance, start_state, jnp.arange(count, dtype=jnp.int32))
    return result


def reference(cond_dens, val_dens, trial_vecs, eig_vals, block_pairs, slot_block):
    nv_bands = val_dens.shape[1]
    nc_bands = cond_dens.shape[1]
    nvec = trial_vecs.shape[2] // nc_bands
    trials = trial_vecs.reshape(trial_vecs.shape[0], nv_bands, nc_bands, nvec)
    image_zero = jnp.zeros((trial_vecs.shape[0] * nv_bands, nc_bands * nvec), jnp.float32)

    def per_slot(image, slot):
        blocknum = slot_block[slot]
        first = block_pairs[blocknum, 0]
        second = block_pairs[blocknum, 1]
        near = trials[first]
        far = trials[second]
        forward, mirror = block_terms(cond_dens[blocknum], val_dens[slot], near, far, eig_vals)
        weight = (first < second).astype(jnp.float32)
        forward = forward.reshape(nv_bands, nc_bands * nvec)
        mirror = weight * mirror.reshape(nv_bands, nc_bands * nvec)
        zero_int = jnp.zeros((), jnp.int32)
        image = image + lax.dynamic_update_slice(jnp.zeros_like(image), forward, ((first * nv_bands).astype(jnp.int32), zero_int))
        image = image + lax.dynamic_update_slice(jnp.zeros_like(image), mirror, ((second * nv_bands).astype(jnp.int32), zero_int))
        return image, None

    image, unused = lax.scan(per_slot, image_zero, jnp.arange(slot_block.shape[0], dtype=jnp.int32))
    return image
```

```python
import functools
import jax
import jax.numpy as jnp
from jax import lax
from jax.experimental import pallas as pl
from jax.experimental.pallas import tpu as pltpu
from jax.sharding import Mesh, PartitionSpec as P

F32 = jnp.float32
BF16 = jnp.bfloat16
MIB = 1024 * 1024


def gather_kernel(first, width, order_ref, cond_ref, out_ref, sem):
    @pl.loop(0, out_ref.shape[0], unroll=8)
    def _(slot):
        pltpu.make_async_copy(
            cond_ref.at[order_ref[slot], :, :, pl.ds(first, width)], out_ref.at[slot], sem
        ).start()

    pltpu.make_async_copy(out_ref, out_ref, sem).wait()


def gather_rows(cond, order, first, width):
    count, one, depth, _ = cond.shape
    shape = (count, one, depth, width)
    return pl.pallas_call(
        functools.partial(gather_kernel, first, width),
        out_shape=jax.ShapeDtypeStruct(shape, cond.dtype),
        grid_spec=pltpu.PrefetchScalarGridSpec(
            num_scalar_prefetch=1,
            grid=(1,),
            in_specs=[pl.BlockSpec(memory_space=pl.ANY)],
            out_specs=pl.BlockSpec(shape, lambda i, order: (0, 0, 0, 0)),
            scratch_shapes=[pltpu.SemaphoreType.DMA],
        ),
        compiler_params=pltpu.CompilerParams(vmem_limit_bytes=60 * MIB),
        cost_estimate=pl.CostEstimate(
            flops=0, bytes_accessed=4 * count * depth * width, transcendentals=0
        ),
        name="gather_rows",
    )(order, cond)


def expand_kernel(nvec, x_ref, v_ref, eig_ref, *out_refs):
    groups = x_ref.shape[0] // nvec
    x = x_ref[...]
    scale = eig_ref[...]
    for pair in range(v_ref.shape[0] // 2):
        low = jnp.dot(x, v_ref[2 * pair], preferred_element_type=F32) * scale
        high = jnp.dot(x, v_ref[2 * pair + 1], preferred_element_type=F32) * scale
        rows = pl.ds(pair * 2 * nvec, 2 * nvec)
        for b in range(groups):
            both = jnp.concatenate(
                [low[b * nvec : (b + 1) * nvec], high[b * nvec : (b + 1) * nvec]], axis=0
            ).astype(BF16)
            start = 0
            for out_ref in out_refs:
                width = out_ref.shape[1] // groups
                out_ref[rows, pl.ds(b * width, width)] = both[:, start : start + width]
                start += width


def expand(x, v, eig, widths, nvec, step):
    count, depth, lanes = v.shape
    rows = x.shape[0]
    groups = rows // nvec
    return pl.pallas_call(
        functools.partial(expand_kernel, nvec),
        out_shape=[
            jax.ShapeDtypeStruct((count * nvec, groups * width), BF16) for width in widths
        ],
        grid=(count // step,),
        in_specs=[
            pl.BlockSpec((rows, depth), lambda i: (0, 0)),
            pl.BlockSpec((step, depth, lanes), lambda i: (i, 0, 0)),
            pl.BlockSpec((1, lanes), lambda i: (0, 0)),
        ],
        out_specs=[
            pl.BlockSpec((step * nvec, groups * width), lambda i: (i, 0)) for width in widths
        ],
        compiler_params=pltpu.CompilerParams(vmem_limit_bytes=60 * MIB),
        cost_estimate=pl.CostEstimate(
            flops=2 * rows * depth * lanes * count,
            bytes_accessed=2 * count * rows * lanes + 2 * count * depth * lanes,
            transcendentals=0,
        ),
        name="expand",
    )(x, v, eig)


def add_products(u_ref, c_ref, acc_ref):
    c = jnp.concatenate([c_ref[j] for j in range(c_ref.shape[0])], axis=1)
    acc_ref[...] += lax.dot_general(
        u_ref[...], c, (((1,), (1,)), ((), ())), preferred_element_type=F32
    )


def first_kernel(u2_ref, ct_ref, u1_ref, c_ref, fwd_ref, mir_ref):
    @pl.when(pl.program_id(0) == 0)
    def _():
        fwd_ref[...] = jnp.zeros_like(fwd_ref)
        mir_ref[...] = jnp.zeros_like(mir_ref)

    add_products(u2_ref, ct_ref, fwd_ref)
    add_products(u1_ref, c_ref, mir_ref)


def last_kernel(u2_ref, ct_ref, u1_ref, c_ref, fwd0_ref, mir0_ref, out_ref, fwd_ref, mir_ref):
    @pl.when(pl.program_id(0) == 0)
    def _():
        fwd_ref[...] = fwd0_ref[...]
        mir_ref[...] = mir0_ref[...]

    add_products(u2_ref, ct_ref, fwd_ref)
    add_products(u1_ref, c_ref, mir_ref)

    @pl.when(pl.program_id(0) == pl.num_programs(0) - 1)
    def _():
        pieces, _, rows, lanes = out_ref.shape
        parts = fwd_ref.shape[1] // rows
        for which, ref in ((0, fwd_ref), (1, mir_ref)):
            flipped = ref[...].T.astype(BF16)
            for piece in range(pieces):
                half, part = piece // parts, piece % parts
                out_ref[piece, which] = flipped[
                    part * rows : (part + 1) * rows, half * lanes : (half + 1) * lanes
                ]


def contract(u2, ct, u1, c, step, before=None, pieces=None):
    rows = u2.shape[0]
    groups, cols, width = c.shape
    u_spec = pl.BlockSpec((rows, step * width), lambda i: (0, i))
    c_spec = pl.BlockSpec((step, cols, width), lambda i: (i, 0, 0))
    sum_spec = pl.BlockSpec((rows, cols), lambda i: (0, 0))
    sums = jax.ShapeDtypeStruct((rows, cols), F32)
    common = dict(
        grid=(groups // step,),
        compiler_params=pltpu.CompilerParams(vmem_limit_bytes=60 * MIB),
        cost_estimate=pl.CostEstimate(
            flops=4 * rows * cols * groups * width,
            bytes_accessed=4 * groups * width * (rows + cols),
            transcendentals=0,
        ),
    )
    if before is None:
        return pl.pallas_call(
            first_kernel,
            out_shape=[sums, sums],
            in_specs=[u_spec, c_spec, u_spec, c_spec],
            out_specs=[sum_spec, sum_spec],
            name="contract_first",
            **common,
        )(u2, ct, u1, c)
    return pl.pallas_call(
        last_kernel,
        out_shape=jax.ShapeDtypeStruct(pieces, BF16),
        in_specs=[u_spec, c_spec, u_spec, c_spec, sum_spec, sum_spec],
        out_specs=pl.BlockSpec(pieces, lambda i: (0, 0, 0, 0)),
        scratch_shapes=[pltpu.VMEM((rows, cols), F32), pltpu.VMEM((rows, cols), F32)],
        name="contract_last",
        **common,
    )(u2, ct, u1, c, *before)


def per_device(cond_dens, val_dens, trial_vecs, eig_vals, block_pairs, slot_block):
    kpoints, nv_bands, columns = trial_vecs.shape
    nc_bands = cond_dens.shape[2]
    nvec = columns // nc_bands
    lanes = cond_dens.shape[3]
    cores, eigs = lax.axis_size("c"), lax.axis_size("x")
    chip = lax.axis_index("z") * lax.axis_size("y") + lax.axis_index("y")
    slot = chip * cores + lax.axis_index("c")
    kp = ("z", "y", "c")

    late = 128
    early = lanes - late
    sent_early = gather_rows(cond_dens, slot_block, 0, early)
    owned_early = lax.all_to_all(sent_early, kp, split_axis=0, concat_axis=0, tiled=True)
    pair = block_pairs[slot_block[slot]]
    near = trial_vecs[pair[0]] * (pair[0] < pair[1]).astype(BF16)
    far = trial_vecs[pair[1]]
    near = near.reshape(nv_bands, columns).T
    far = far.reshape(nv_bands, columns).T
    eig = eig_vals[None, :]
    values = val_dens[0]
    u2_early, u2_late = expand(far, values, eig, (early, late), nvec, 4)
    u1_early, u1_late = expand(near, values.transpose(1, 0, 2), eig, (early, late), nvec, 4)

    sent_late = gather_rows(cond_dens, slot_block, early, late)
    sent_late, owned_early, u2_early, u2_late, u1_early, u1_late = lax.optimization_barrier(
        (sent_late, owned_early, u2_early, u2_late, u1_early, u1_late)
    )
    owned_late = lax.all_to_all(sent_late, kp, split_axis=0, concat_axis=0, tiled=True)
    owned_early = owned_early.reshape(nc_bands, nc_bands, early)
    owned_late = owned_late.reshape(nc_bands, nc_bands, late)

    before = contract(u2_early, owned_early.transpose(1, 0, 2), u1_early, owned_early, 4)
    part_rows = nc_bands // eigs
    half_lanes = nv_bands * nvec // cores
    pieces = (cores * eigs, 2, part_rows, half_lanes)
    sums = contract(
        u2_late, owned_late.transpose(1, 0, 2), u1_late, owned_late, 8, before, pieces
    )

    arrived = lax.all_to_all(sums, ("c", "x"), split_axis=0, concat_axis=0, tiled=True)
    arrived = arrived.reshape(cores, eigs, 2, part_rows, half_lanes).astype(F32).sum(1)
    kpoint = jnp.arange(kpoints, dtype=jnp.int32)
    placed = jnp.zeros((kpoints, part_rows, half_lanes), F32)
    for core in range(cores):
        both = block_pairs[slot_block[chip * cores + core]]
        for which in range(2):
            hit = (kpoint == both[which])[:, None, None]
            placed = placed + jnp.where(hit, arrived[core, which][None], 0.0)
    image = lax.all_to_all(placed.astype(BF16), ("z", "y"), split_axis=0, concat_axis=0, tiled=True)
    image = image.astype(F32).sum(0).reshape(part_rows, nv_bands // cores, nvec)
    return image.transpose(1, 0, 2).reshape(nv_bands // cores, part_rows * nvec)


def solution(mesh):
    kp, eig = mesh.devices.shape
    fine = Mesh(mesh.devices.reshape(8, kp // 16, 2, eig), ("z", "y", "c", "x"))
    kp_axes = ("z", "y", "c")
    return jax.shard_map(
        per_device,
        mesh=fine,
        in_specs=(
            P(None, kp_axes, None, "x"),
            P(kp_axes, None, None, "x"),
            P(),
            P("x"),
            P(),
            P(),
        ),
        out_specs=P(kp_axes, "x"),
        check_vma=False,
    )
```

```python
import functools
import jax
import jax.numpy as jnp
from jax import lax
from jax.experimental import pallas as pl
from jax.experimental.pallas import tpu as pltpu
from jax.sharding import Mesh, PartitionSpec as P

F32 = jnp.float32
BF16 = jnp.bfloat16
MIB = 1024 * 1024


def gather_kernel(first, width, chunks, order_ref, cond_ref, out_ref, held, in_sems, out_sems):
    size = held.shape[0] // chunks

    for chunk in range(chunks):
        @pl.loop(chunk * size, (chunk + 1) * size, unroll=8)
        def _(slot):
            pltpu.make_async_copy(
                cond_ref.at[order_ref[slot], :, :, pl.ds(first, width)],
                held.at[slot],
                in_sems.at[chunk],
            ).start()

    stores = []
    for chunk in range(chunks):
        part = pl.ds(chunk * size, size)
        pltpu.make_async_copy(held.at[part], held.at[part], in_sems.at[chunk]).wait()
        stores.append(pltpu.make_async_copy(held.at[part], out_ref.at[part], out_sems.at[chunk]))
        stores[-1].start()
    for store in stores:
        store.wait()


def gather_rows(cond, order, first, width, chunks):
    count, one, depth, _ = cond.shape
    shape = (count, one, depth, width)
    return pl.pallas_call(
        functools.partial(gather_kernel, first, width, chunks),
        out_shape=jax.ShapeDtypeStruct(shape, cond.dtype),
        in_specs=[pl.BlockSpec(memory_space=pltpu.SMEM), pl.BlockSpec(memory_space=pl.ANY)],
        out_specs=pl.BlockSpec(memory_space=pl.ANY),
        scratch_shapes=[
            pltpu.VMEM(shape, cond.dtype),
            pltpu.SemaphoreType.DMA((chunks,)),
            pltpu.SemaphoreType.DMA((chunks,)),
        ],
        compiler_params=pltpu.CompilerParams(vmem_limit_bytes=60 * MIB),
        cost_estimate=pl.CostEstimate(
            flops=0, bytes_accessed=4 * count * depth * width, transcendentals=0
        ),
        name="gather_rows",
    )(order, cond)


def expand_kernel(nvec, x_ref, v_ref, eig_ref, *out_refs):
    groups = x_ref.shape[0] // nvec
    x = x_ref[...]
    scale = eig_ref[...]
    for pair in range(v_ref.shape[0] // 2):
        low = jnp.dot(x, v_ref[2 * pair], preferred_element_type=F32) * scale
        high = jnp.dot(x, v_ref[2 * pair + 1], preferred_element_type=F32) * scale
        rows = pl.ds(pair * 2 * nvec, 2 * nvec)
        for b in range(groups):
            both = jnp.concatenate(
                [low[b * nvec : (b + 1) * nvec], high[b * nvec : (b + 1) * nvec]], axis=0
            ).astype(BF16)
            start = 0
            for out_ref in out_refs:
                width = out_ref.shape[1] // groups
                out_ref[rows, pl.ds(b * width, width)] = both[:, start : start + width]
                start += width


def expand(x, v, eig, widths, nvec, step):
    count, depth, lanes = v.shape
    rows = x.shape[0]
    groups = rows // nvec
    return pl.pallas_call(
        functools.partial(expand_kernel, nvec),
        out_shape=[
            jax.ShapeDtypeStruct((count * nvec, groups * width), BF16) for width in widths
        ],
        grid=(count // step,),
        in_specs=[
            pl.BlockSpec((rows, depth), lambda i: (0, 0)),
            pl.BlockSpec((step, depth, lanes), lambda i: (i, 0, 0)),
            pl.BlockSpec((1, lanes), lambda i: (0, 0)),
        ],
        out_specs=[
            pl.BlockSpec((step * nvec, groups * width), lambda i: (i, 0)) for width in widths
        ],
        compiler_params=pltpu.CompilerParams(vmem_limit_bytes=60 * MIB),
        cost_estimate=pl.CostEstimate(
            flops=2 * rows * depth * lanes * count,
            bytes_accessed=2 * count * rows * lanes + 2 * count * depth * lanes,
            transcendentals=0,
        ),
        name="expand",
    )(x, v, eig)


def product(c, u):
    return lax.dot_general(c, u, (((1,), (1,)), ((), ())), preferred_element_type=F32)


def first_kernel(u2_ref, ct_ref, u1_ref, c_ref, fwd_ref, mir_ref):
    @pl.when(pl.program_id(0) == 0)
    def _():
        fwd_ref[...] = jnp.zeros_like(fwd_ref)
        mir_ref[...] = jnp.zeros_like(mir_ref)

    for u_ref, rows_ref, sum_ref in ((u2_ref, ct_ref, fwd_ref), (u1_ref, c_ref, mir_ref)):
        rows = jnp.concatenate([rows_ref[j] for j in range(rows_ref.shape[0])], axis=1)
        sum_ref[...] += product(rows, u_ref[...])


def contract_first(u2, ct, u1, c, step):
    rows = u2.shape[0]
    groups, cols, width = c.shape
    u_spec = pl.BlockSpec((rows, step * width), lambda i: (0, i))
    c_spec = pl.BlockSpec((step, cols, width), lambda i: (i, 0, 0))
    sum_spec = pl.BlockSpec((cols, rows), lambda i: (0, 0))
    sums = jax.ShapeDtypeStruct((cols, rows), F32)
    return pl.pallas_call(
        first_kernel,
        out_shape=[sums, sums],
        grid=(groups // step,),
        in_specs=[u_spec, c_spec, u_spec, c_spec],
        out_specs=[sum_spec, sum_spec],
        compiler_params=pltpu.CompilerParams(vmem_limit_bytes=60 * MIB),
        cost_estimate=pl.CostEstimate(
            flops=4 * rows * cols * groups * width,
            bytes_accessed=4 * groups * width * (rows + cols),
            transcendentals=0,
        ),
        name="contract_first",
    )(u2, ct, u1, c)


def last_kernel(
    step, ahead, pad, u2_ref, u1_ref, c_hbm, fwd_ref, mir_ref, out_ref, c_ref, u_ref, flip, c_sem, u_sems
):
    groups, cols, width = c_ref.shape
    blocks = groups // step
    lanes = step * width
    fetch_c = pltpu.make_async_copy(c_hbm, c_ref, c_sem)
    fetches = [
        pltpu.make_async_copy(
            source.at[:, pl.ds(block * lanes, lanes)],
            u_ref.at[which * blocks + block],
            u_sems.at[which * blocks + block],
        )
        for which, source in ((0, u1_ref), (1, u2_ref))
        for block in range(blocks)
    ]
    fetch_c.start()
    for index in range(ahead):
        fetches[index].start()

    def arrived(index):
        fetches[index].wait()
        if index + ahead < len(fetches):
            fetches[index + ahead].start()
        return u_ref[index]

    fetch_c.wait()
    for c in range(groups):
        flip[pl.ds(c * pad, cols)] = c_ref[c].astype(F32)
    forward, mirror = fwd_ref[...], mir_ref[...]
    for block in range(blocks):
        rows = jnp.concatenate([c_ref[block * step + j] for j in range(step)], axis=1)
        mirror = mirror + product(rows, arrived(block))
    for block in range(blocks):
        rows = jnp.concatenate(
            [
                flip[pl.ds(block * step + j, groups, stride=pad)].astype(BF16)
                for j in range(step)
            ],
            axis=1,
        )
        forward = forward + product(rows, arrived(blocks + block))
    pieces, _, part, half_lanes = out_ref.shape
    parts = cols // part
    for which, total in ((0, forward), (1, mirror)):
        total = total.astype(BF16)
        for piece in range(pieces):
            half, eig = piece // parts, piece % parts
            out_ref[piece, which] = total[
                eig * part : (eig + 1) * part, half * half_lanes : (half + 1) * half_lanes
            ]


def contract_last(u2, u1, c, forward, mirror, pieces, step, ahead):
    rows = u2.shape[0]
    groups, cols, width = c.shape
    pad = cols + 8
    copies = 2 * groups // step
    whole = pl.BlockSpec(memory_space=pltpu.VMEM)
    away = pl.BlockSpec(memory_space=pl.ANY)
    return pl.pallas_call(
        functools.partial(last_kernel, step, ahead, pad),
        out_shape=jax.ShapeDtypeStruct(pieces, BF16),
        in_specs=[away, away, away, whole, whole],
        out_specs=whole,
        scratch_shapes=[
            pltpu.VMEM((groups, cols, width), BF16),
            pltpu.VMEM((copies, rows, step * width), BF16),
            pltpu.VMEM((groups * pad, width), F32),
            pltpu.SemaphoreType.DMA,
            pltpu.SemaphoreType.DMA((copies,)),
        ],
        compiler_params=pltpu.CompilerParams(vmem_limit_bytes=60 * MIB),
        cost_estimate=pl.CostEstimate(
            flops=4 * rows * cols * groups * width,
            bytes_accessed=4 * groups * width * (rows + cols),
            transcendentals=0,
        ),
        name="contract_last",
    )(u2, u1, c, forward, mirror)


def per_device(cond_dens, val_dens, trial_vecs, eig_vals, block_pairs, slot_block):
    kpoints, nv_bands, columns = trial_vecs.shape
    nc_bands = cond_dens.shape[2]
    nvec = columns // nc_bands
    lanes = cond_dens.shape[3]
    cores, eigs = lax.axis_size("c"), lax.axis_size("x")
    chip = lax.axis_index("z") * lax.axis_size("y") + lax.axis_index("y")
    slot = chip * cores + lax.axis_index("c")
    kp = ("z", "y", "c")

    late = 128
    early = lanes - late
    sent_early = gather_rows(cond_dens, slot_block, 0, early, 4)
    owned_early = lax.all_to_all(sent_early, kp, split_axis=0, concat_axis=0, tiled=True)
    pair = block_pairs[slot_block[slot]]
    near = trial_vecs[pair[0]] * (pair[0] < pair[1]).astype(BF16)
    far = trial_vecs[pair[1]]
    near = near.reshape(nv_bands, columns).T
    far = far.reshape(nv_bands, columns).T
    eig = eig_vals[None, :]
    values = val_dens[0]
    u2_early, u2_late = expand(far, values, eig, (early, late), nvec, 4)
    u1_early, u1_late = expand(near, values.transpose(1, 0, 2), eig, (early, late), nvec, 4)

    sent_late = gather_rows(cond_dens, slot_block, early, late, 2)
    both = block_pairs[lax.dynamic_slice_in_dim(slot_block, chip * cores, cores)]
    hits = (jnp.arange(kpoints, dtype=jnp.int32) == both[:, :, None]).astype(F32)
    sent_late, owned_early, u2_early, u1_early, hits = lax.optimization_barrier(
        (sent_late, owned_early, u2_early, u1_early, hits)
    )
    owned_late = lax.all_to_all(sent_late, kp, split_axis=0, concat_axis=0, tiled=True)
    owned_early = owned_early.reshape(nc_bands, nc_bands, early)
    owned_late = owned_late.reshape(nc_bands, nc_bands, late)

    forward, mirror = contract_first(
        u2_early, owned_early.transpose(1, 0, 2), u1_early, owned_early, 8
    )
    part_rows = nc_bands // eigs
    half_lanes = nv_bands * nvec // cores
    pieces = (cores * eigs, 2, part_rows, half_lanes)
    sums = contract_last(u2_late, u1_late, owned_late, forward, mirror, pieces, 8, 4)

    arrived = lax.all_to_all(sums, ("c", "x"), split_axis=0, concat_axis=0, tiled=True)
    arrived = arrived.reshape(cores, eigs, 2, part_rows, half_lanes).astype(F32).sum(1)
    placed = jnp.zeros((kpoints, part_rows, half_lanes), F32)
    for core in range(cores):
        for which in range(2):
            placed = placed + hits[core, which][:, None, None] * arrived[core, which]
    image = lax.all_to_all(placed.astype(BF16), ("z", "y"), split_axis=0, concat_axis=0, tiled=True)
    image = image.astype(F32).sum(0).reshape(part_rows, nv_bands // cores, nvec)
    return image.transpose(1, 0, 2).reshape(nv_bands // cores, part_rows * nvec)


def solution(mesh):
    kp, eig = mesh.devices.shape
    fine = Mesh(mesh.devices.reshape(8, kp // 16, 2, eig), ("z", "y", "c", "x"))
    kp_axes = ("z", "y", "c")
    return jax.shard_map(
        per_device,
        mesh=fine,
        in_specs=(
            P(None, kp_axes, None, "x"),
            P(kp_axes, None, None, "x"),
            P(),
            P("x"),
            P(),
            P(),
        ),
        out_specs=P(kp_axes, "x"),
        check_vma=False,
    )
```

```python
import functools
import jax
import jax.numpy as jnp
from jax import lax
from jax.experimental import pallas as pl
from jax.experimental.pallas import tpu as pltpu
from jax.sharding import Mesh, PartitionSpec as P

F32 = jnp.float32
BF16 = jnp.bfloat16
MIB = 1024 * 1024


def gather_kernel(first, width, chunks, order_ref, cond_ref, out_ref, held, in_sems, out_sems):
    size = held.shape[0] // chunks

    for chunk in range(chunks):
        @pl.loop(chunk * size, (chunk + 1) * size, unroll=8)
        def _(slot):
            pltpu.make_async_copy(
                cond_ref.at[order_ref[slot], :, :, pl.ds(first, width)],
                held.at[slot],
                in_sems.at[chunk],
            ).start()

    stores = []
    for chunk in range(chunks):
        part = pl.ds(chunk * size, size)
        pltpu.make_async_copy(held.at[part], held.at[part], in_sems.at[chunk]).wait()
        stores.append(pltpu.make_async_copy(held.at[part], out_ref.at[part], out_sems.at[chunk]))
        stores[-1].start()
    for store in stores:
        store.wait()


def gather_rows(cond, order, first, width, chunks):
    count, one, depth, _ = cond.shape
    shape = (count, one, depth, width)
    return pl.pallas_call(
        functools.partial(gather_kernel, first, width, chunks),
        out_shape=jax.ShapeDtypeStruct(shape, cond.dtype),
        in_specs=[pl.BlockSpec(memory_space=pltpu.SMEM), pl.BlockSpec(memory_space=pl.ANY)],
        out_specs=pl.BlockSpec(memory_space=pl.ANY),
        scratch_shapes=[
            pltpu.VMEM(shape, cond.dtype),
            pltpu.SemaphoreType.DMA((chunks,)),
            pltpu.SemaphoreType.DMA((chunks,)),
        ],
        compiler_params=pltpu.CompilerParams(vmem_limit_bytes=60 * MIB),
        cost_estimate=pl.CostEstimate(
            flops=0, bytes_accessed=4 * count * depth * width, transcendentals=0
        ),
        name="gather_rows",
    )(order, cond)


def expand_kernel(nvec, x_ref, v_ref, eig_ref, *out_refs):
    groups = x_ref.shape[0] // nvec
    x = x_ref[...]
    scale = eig_ref[...]
    for pair in range(v_ref.shape[0] // 2):
        low = jnp.dot(x, v_ref[2 * pair], preferred_element_type=F32) * scale
        high = jnp.dot(x, v_ref[2 * pair + 1], preferred_element_type=F32) * scale
        rows = pl.ds(pair * 2 * nvec, 2 * nvec)
        for b in range(groups):
            both = jnp.concatenate(
                [low[b * nvec : (b + 1) * nvec], high[b * nvec : (b + 1) * nvec]], axis=0
            ).astype(BF16)
            start = 0
            for out_ref in out_refs:
                width = out_ref.shape[1] // groups
                out_ref[rows, pl.ds(b * width, width)] = both[:, start : start + width]
                start += width


def expand(x, v, eig, widths, nvec, step):
    count, depth, lanes = v.shape
    rows = x.shape[0]
    groups = rows // nvec
    return pl.pallas_call(
        functools.partial(expand_kernel, nvec),
        out_shape=[
            jax.ShapeDtypeStruct((count * nvec, groups * width), BF16) for width in widths
        ],
        grid=(count // step,),
        in_specs=[
            pl.BlockSpec((rows, depth), lambda i: (0, 0)),
            pl.BlockSpec((step, depth, lanes), lambda i: (i, 0, 0)),
            pl.BlockSpec((1, lanes), lambda i: (0, 0)),
        ],
        out_specs=[
            pl.BlockSpec((step * nvec, groups * width), lambda i: (i, 0)) for width in widths
        ],
        compiler_params=pltpu.CompilerParams(vmem_limit_bytes=60 * MIB),
        cost_estimate=pl.CostEstimate(
            flops=2 * rows * depth * lanes * count,
            bytes_accessed=2 * count * rows * lanes + 2 * count * depth * lanes,
            transcendentals=0,
        ),
        name="expand",
    )(x, v, eig)


def product(c, u):
    return lax.dot_general(c, u, (((1,), (1,)), ((), ())), preferred_element_type=F32)


def first_kernel(u2_ref, ct_ref, u1_ref, c_ref, fwd_ref, mir_ref):
    @pl.when(pl.program_id(0) == 0)
    def _():
        fwd_ref[...] = jnp.zeros_like(fwd_ref)
        mir_ref[...] = jnp.zeros_like(mir_ref)

    for u_ref, rows_ref, sum_ref in ((u2_ref, ct_ref, fwd_ref), (u1_ref, c_ref, mir_ref)):
        rows = jnp.concatenate([rows_ref[j] for j in range(rows_ref.shape[0])], axis=1)
        sum_ref[...] += product(rows, u_ref[...])


def contract_first(u2, ct, u1, c, step):
    rows = u2.shape[0]
    groups, cols, width = c.shape
    u_spec = pl.BlockSpec((rows, step * width), lambda i: (0, i))
    c_spec = pl.BlockSpec((step, cols, width), lambda i: (i, 0, 0))
    sum_spec = pl.BlockSpec((cols, rows), lambda i: (0, 0))
    sums = jax.ShapeDtypeStruct((cols, rows), F32)
    return pl.pallas_call(
        first_kernel,
        out_shape=[sums, sums],
        grid=(groups // step,),
        in_specs=[u_spec, c_spec, u_spec, c_spec],
        out_specs=[sum_spec, sum_spec],
        compiler_params=pltpu.CompilerParams(vmem_limit_bytes=60 * MIB),
        cost_estimate=pl.CostEstimate(
            flops=4 * rows * cols * groups * width,
            bytes_accessed=4 * groups * width * (rows + cols),
            transcendentals=0,
        ),
        name="contract_first",
    )(u2, ct, u1, c)


def last_kernel(
    step, ahead, pad, u2_hbm, u1_hbm, c_hbm, fwd_hbm, mir_hbm, out_hbm,
    c_ref, u_ref, flip, fwd_ref, mir_ref, fwd_out, mir_out, c_sem, u_sems, sum_sems, out_sems,
):
    groups, cols, width = c_ref.shape
    blocks = groups // step
    lanes = step * width
    fetch_c = pltpu.make_async_copy(c_hbm, c_ref, c_sem)
    fetch_mir = pltpu.make_async_copy(mir_hbm, mir_ref, sum_sems.at[0])
    fetch_fwd = pltpu.make_async_copy(fwd_hbm, fwd_ref, sum_sems.at[1])
    fetches = [
        pltpu.make_async_copy(
            source.at[:, pl.ds(block * lanes, lanes)],
            u_ref.at[which * blocks + block],
            u_sems.at[which * blocks + block],
        )
        for which, source in ((0, u1_hbm), (1, u2_hbm))
        for block in range(blocks)
    ]
    fetch_c.start()
    for index in range(2):
        fetches[index].start()
    fetch_c.wait()
    for index in range(2, ahead):
        fetches[index].start()
    fetch_mir.start()
    fetch_fwd.start()

    def arrived(index):
        fetches[index].wait()
        if index + ahead < len(fetches):
            fetches[index + ahead].start()
        return u_ref[index]

    def leave(total, pieces_ref, which):
        total = total.astype(BF16)
        pieces, part, half_lanes = pieces_ref.shape
        parts = cols // part
        for piece in range(pieces):
            half, eig = piece // parts, piece % parts
            pieces_ref[piece] = total[
                eig * part : (eig + 1) * part, half * half_lanes : (half + 1) * half_lanes
            ]
        copy = pltpu.make_async_copy(pieces_ref, out_hbm.at[:, which], out_sems.at[which])
        copy.start()
        return copy

    total = jnp.zeros(mir_ref.shape, F32)
    for block in range(blocks):
        rows = jnp.concatenate([c_ref[block * step + j] for j in range(step)], axis=1)
        total = total + product(rows, arrived(block))
    fetch_mir.wait()
    mirror_left = leave(total + mir_ref[...], mir_out, 1)

    for c in range(groups):
        flip[pl.ds(c * pad, cols)] = c_ref[c].astype(F32)
    total = jnp.zeros(fwd_ref.shape, F32)
    for block in range(blocks):
        rows = jnp.concatenate(
            [
                flip[pl.ds(block * step + j, groups, stride=pad)].astype(BF16)
                for j in range(step)
            ],
            axis=1,
        )
        total = total + product(rows, arrived(blocks + block))
    fetch_fwd.wait()
    forward_left = leave(total + fwd_ref[...], fwd_out, 0)
    mirror_left.wait()
    forward_left.wait()


def contract_last(u2, u1, c, forward, mirror, pieces, step, ahead):
    rows = u2.shape[0]
    groups, cols, width = c.shape
    pad = cols + 8
    copies = 2 * groups // step
    away = pl.BlockSpec(memory_space=pl.ANY)
    one_way = (pieces[0],) + pieces[2:]
    return pl.pallas_call(
        functools.partial(last_kernel, step, ahead, pad),
        out_shape=jax.ShapeDtypeStruct(pieces, BF16),
        in_specs=[away] * 5,
        out_specs=away,
        scratch_shapes=[
            pltpu.VMEM((groups, cols, width), BF16),
            pltpu.VMEM((copies, rows, step * width), BF16),
            pltpu.VMEM((groups * pad, width), F32),
            pltpu.VMEM(forward.shape, F32),
            pltpu.VMEM(mirror.shape, F32),
            pltpu.VMEM(one_way, BF16),
            pltpu.VMEM(one_way, BF16),
            pltpu.SemaphoreType.DMA,
            pltpu.SemaphoreType.DMA((copies,)),
            pltpu.SemaphoreType.DMA((2,)),
            pltpu.SemaphoreType.DMA((2,)),
        ],
        compiler_params=pltpu.CompilerParams(vmem_limit_bytes=60 * MIB),
        cost_estimate=pl.CostEstimate(
            flops=4 * rows * cols * groups * width,
            bytes_accessed=4 * groups * width * (rows + cols),
            transcendentals=0,
        ),
        name="contract_last",
    )(u2, u1, c, forward, mirror)


def per_device(cond_dens, val_dens, trial_vecs, eig_vals, block_pairs, slot_block):
    kpoints, nv_bands, columns = trial_vecs.shape
    nc_bands = cond_dens.shape[2]
    nvec = columns // nc_bands
    lanes = cond_dens.shape[3]
    cores, eigs = lax.axis_size("c"), lax.axis_size("x")
    chip = lax.axis_index("z") * lax.axis_size("y") + lax.axis_index("y")
    slot = chip * cores + lax.axis_index("c")
    kp = ("z", "y", "c")

    late = 128
    early = lanes - late
    sent_early = gather_rows(cond_dens, slot_block, 0, early, 4)
    owned_early = lax.all_to_all(sent_early, kp, split_axis=0, concat_axis=0, tiled=True)
    pair = block_pairs[slot_block[slot]]
    near = trial_vecs[pair[0]] * (pair[0] < pair[1]).astype(BF16)
    far = trial_vecs[pair[1]]
    near = near.reshape(nv_bands, columns).T
    far = far.reshape(nv_bands, columns).T
    eig = eig_vals[None, :]
    values = val_dens[0]
    u2_early, u2_late = expand(far, values, eig, (early, late), nvec, 4)
    u1_early, u1_late = expand(near, values.transpose(1, 0, 2), eig, (early, late), nvec, 4)

    sent_late = gather_rows(cond_dens, slot_block, early, late, 2)
    both = block_pairs[lax.dynamic_slice_in_dim(slot_block, chip * cores, cores)]
    hits = (jnp.arange(kpoints, dtype=jnp.int32) == both[:, :, None]).astype(F32)
    sent_late, owned_early, u2_early, u1_early, hits = lax.optimization_barrier(
        (sent_late, owned_early, u2_early, u1_early, hits)
    )
    owned_late = lax.all_to_all(sent_late, kp, split_axis=0, concat_axis=0, tiled=True)
    owned_early = owned_early.reshape(nc_bands, nc_bands, early)
    owned_late = owned_late.reshape(nc_bands, nc_bands, late)

    forward, mirror = contract_first(
        u2_early, owned_early.transpose(1, 0, 2), u1_early, owned_early, 8
    )
    part_rows = nc_bands // eigs
    half_lanes = nv_bands * nvec // cores
    pieces = (cores * eigs, 2, part_rows, half_lanes)
    sums = contract_last(u2_late, u1_late, owned_late, forward, mirror, pieces, 8, 6)

    arrived = lax.all_to_all(sums, ("c", "x"), split_axis=0, concat_axis=0, tiled=True)
    arrived = arrived.reshape(cores, eigs, 2, part_rows, half_lanes).astype(F32).sum(1)
    placed = jnp.zeros((kpoints, part_rows, half_lanes), F32)
    for core in range(cores):
        for which in range(2):
            placed = placed + hits[core, which][:, None, None] * arrived[core, which]
    image = lax.all_to_all(placed.astype(BF16), ("z", "y"), split_axis=0, concat_axis=0, tiled=True)
    image = image.astype(F32).sum(0).reshape(part_rows, nv_bands // cores, nvec)
    return image.transpose(1, 0, 2).reshape(nv_bands // cores, part_rows * nvec)


def solution(mesh):
    kp, eig = mesh.devices.shape
    fine = Mesh(mesh.devices.reshape(8, kp // 16, 2, eig), ("z", "y", "c", "x"))
    kp_axes = ("z", "y", "c")
    return jax.shard_map(
        per_device,
        mesh=fine,
        in_specs=(
            P(None, kp_axes, None, "x"),
            P(kp_axes, None, None, "x"),
            P(),
            P("x"),
            P(),
            P(),
        ),
        out_specs=P(kp_axes, "x"),
        check_vma=False,
    )
```

```python
import functools
import jax
import jax.numpy as jnp
from jax import lax
from jax.experimental import pallas as pl
from jax.experimental.pallas import tpu as pltpu
from jax.sharding import Mesh, PartitionSpec as P

F32 = jnp.float32
BF16 = jnp.bfloat16
MIB = 1024 * 1024


def gather_kernel(first, width, chunks, order_ref, cond_ref, out_ref, held, in_sems, out_sems):
    size = held.shape[0] // chunks

    for chunk in range(chunks):
        @pl.loop(chunk * size, (chunk + 1) * size, unroll=8)
        def _(slot):
            pltpu.make_async_copy(
                cond_ref.at[order_ref[slot], :, :, pl.ds(first, width)],
                held.at[slot],
                in_sems.at[chunk],
            ).start()

    stores = []
    for chunk in range(chunks):
        part = pl.ds(chunk * size, size)
        pltpu.make_async_copy(held.at[part], held.at[part], in_sems.at[chunk]).wait()
        stores.append(pltpu.make_async_copy(held.at[part], out_ref.at[part], out_sems.at[chunk]))
        stores[-1].start()
    for store in stores:
        store.wait()


def gather_rows(cond, order, first, width, chunks):
    count, one, depth, _ = cond.shape
    shape = (count, one, depth, width)
    return pl.pallas_call(
        functools.partial(gather_kernel, first, width, chunks),
        out_shape=jax.ShapeDtypeStruct(shape, cond.dtype),
        in_specs=[pl.BlockSpec(memory_space=pltpu.SMEM), pl.BlockSpec(memory_space=pl.ANY)],
        out_specs=pl.BlockSpec(memory_space=pl.ANY),
        scratch_shapes=[
            pltpu.VMEM(shape, cond.dtype),
            pltpu.SemaphoreType.DMA((chunks,)),
            pltpu.SemaphoreType.DMA((chunks,)),
        ],
        compiler_params=pltpu.CompilerParams(vmem_limit_bytes=60 * MIB),
        cost_estimate=pl.CostEstimate(
            flops=0, bytes_accessed=4 * count * depth * width, transcendentals=0
        ),
        name="gather_rows",
    )(order, cond)


def expand_kernel(nvec, x_ref, v_ref, eig_ref, *out_refs):
    groups = x_ref.shape[0] // nvec
    x = x_ref[...]
    scale = eig_ref[...]
    for pair in range(v_ref.shape[0] // 2):
        low = jnp.dot(x, v_ref[2 * pair], preferred_element_type=F32) * scale
        high = jnp.dot(x, v_ref[2 * pair + 1], preferred_element_type=F32) * scale
        rows = pl.ds(pair * 2 * nvec, 2 * nvec)
        for b in range(groups):
            both = jnp.concatenate(
                [low[b * nvec : (b + 1) * nvec], high[b * nvec : (b + 1) * nvec]], axis=0
            ).astype(BF16)
            start = 0
            for out_ref in out_refs:
                width = out_ref.shape[1] // groups
                out_ref[rows, pl.ds(b * width, width)] = both[:, start : start + width]
                start += width


def expand(x, v, eig, widths, nvec, step):
    count, depth, lanes = v.shape
    rows = x.shape[0]
    groups = rows // nvec
    return pl.pallas_call(
        functools.partial(expand_kernel, nvec),
        out_shape=[
            jax.ShapeDtypeStruct((count * nvec, groups * width), BF16) for width in widths
        ],
        grid=(count // step,),
        in_specs=[
            pl.BlockSpec((rows, depth), lambda i: (0, 0)),
            pl.BlockSpec((step, depth, lanes), lambda i: (i, 0, 0)),
            pl.BlockSpec((1, lanes), lambda i: (0, 0)),
        ],
        out_specs=[
            pl.BlockSpec((step * nvec, groups * width), lambda i: (i, 0)) for width in widths
        ],
        compiler_params=pltpu.CompilerParams(vmem_limit_bytes=60 * MIB),
        cost_estimate=pl.CostEstimate(
            flops=2 * rows * depth * lanes * count,
            bytes_accessed=2 * count * rows * lanes + 2 * count * depth * lanes,
            transcendentals=0,
        ),
        name="expand",
    )(x, v, eig)


def product(c, u):
    return lax.dot_general(c, u, (((1,), (1,)), ((), ())), preferred_element_type=F32)


def first_kernel(u2_ref, ct_ref, u1_ref, c_ref, fwd_ref, mir_ref):
    @pl.when(pl.program_id(0) == 0)
    def _():
        fwd_ref[...] = jnp.zeros_like(fwd_ref)
        mir_ref[...] = jnp.zeros_like(mir_ref)

    for u_ref, rows_ref, sum_ref in ((u2_ref, ct_ref, fwd_ref), (u1_ref, c_ref, mir_ref)):
        rows = jnp.concatenate([rows_ref[j] for j in range(rows_ref.shape[0])], axis=1)
        sum_ref[...] += product(rows, u_ref[...])


def contract_first(u2, ct, u1, c, step):
    rows = u2.shape[0]
    groups, cols, width = c.shape
    u_spec = pl.BlockSpec((rows, step * width), lambda i: (0, i))
    c_spec = pl.BlockSpec((step, cols, width), lambda i: (i, 0, 0))
    sum_spec = pl.BlockSpec((cols, rows), lambda i: (0, 0))
    sums = jax.ShapeDtypeStruct((cols, rows), F32)
    return pl.pallas_call(
        first_kernel,
        out_shape=[sums, sums],
        grid=(groups // step,),
        in_specs=[u_spec, c_spec, u_spec, c_spec],
        out_specs=[sum_spec, sum_spec],
        compiler_params=pltpu.CompilerParams(vmem_limit_bytes=60 * MIB),
        cost_estimate=pl.CostEstimate(
            flops=4 * rows * cols * groups * width,
            bytes_accessed=4 * groups * width * (rows + cols),
            transcendentals=0,
        ),
        name="contract_first",
    )(u2, ct, u1, c)


def last_kernel(
    step, ahead, pad, u2_hbm, u1_hbm, c_hbm, fwd_hbm, mir_hbm, out_hbm,
    c_ref, u_ref, flip, fwd_ref, mir_ref, fwd_out, mir_out, c_sem, u_sems, sum_sems, out_sems,
):
    groups, cols, width = c_ref.shape
    blocks = groups // step
    lanes = step * width
    fetch_c = pltpu.make_async_copy(c_hbm, c_ref, c_sem)
    fetch_mir = pltpu.make_async_copy(mir_hbm, mir_ref, sum_sems.at[0])
    fetch_fwd = pltpu.make_async_copy(fwd_hbm, fwd_ref, sum_sems.at[1])
    fetches = [
        pltpu.make_async_copy(
            source.at[:, pl.ds(block * lanes, lanes)],
            u_ref.at[which * blocks + block],
            u_sems.at[which * blocks + block],
        )
        for which, source in ((0, u1_hbm), (1, u2_hbm))
        for block in range(blocks)
    ]
    fetch_c.start()
    for index in range(2):
        fetches[index].start()
    fetch_c.wait()
    for index in range(2, ahead):
        fetches[index].start()
    fetch_mir.start()
    fetch_fwd.start()

    def arrived(index):
        fetches[index].wait()
        if index + ahead < len(fetches):
            fetches[index + ahead].start()
        return u_ref[index]

    def leave(total, pieces_ref, which):
        total = total.astype(BF16)
        pieces, part, half_lanes = pieces_ref.shape
        parts = cols // part
        for piece in range(pieces):
            half, eig = piece // parts, piece % parts
            pieces_ref[piece] = total[
                eig * part : (eig + 1) * part, half * half_lanes : (half + 1) * half_lanes
            ]
        copy = pltpu.make_async_copy(pieces_ref, out_hbm.at[:, which], out_sems.at[which])
        copy.start()
        return copy

    total = jnp.zeros(mir_ref.shape, F32)
    for block in range(blocks):
        rows = jnp.concatenate([c_ref[block * step + j] for j in range(step)], axis=1)
        total = total + product(rows, arrived(block))
    fetch_mir.wait()
    mirror_left = leave(total + mir_ref[...], mir_out, 1)

    for c in range(groups):
        flip[pl.ds(c * pad, cols)] = c_ref[c].astype(F32)
    total = jnp.zeros(fwd_ref.shape, F32)
    for block in range(blocks):
        rows = jnp.concatenate(
            [
                flip[pl.ds(block * step + j, groups, stride=pad)].astype(BF16)
                for j in range(step)
            ],
            axis=1,
        )
        total = total + product(rows, arrived(blocks + block))
    fetch_fwd.wait()
    forward_left = leave(total + fwd_ref[...], fwd_out, 0)
    mirror_left.wait()
    forward_left.wait()


def contract_last(u2, u1, c, forward, mirror, pieces, step, ahead):
    rows = u2.shape[0]
    groups, cols, width = c.shape
    pad = cols + 8
    copies = 2 * groups // step
    away = pl.BlockSpec(memory_space=pl.ANY)
    one_way = (pieces[0],) + pieces[2:]
    return pl.pallas_call(
        functools.partial(last_kernel, step, ahead, pad),
        out_shape=pltpu.VMEM(pieces, BF16),
        in_specs=[away] * 5,
        out_specs=away,
        scratch_shapes=[
            pltpu.VMEM((groups, cols, width), BF16),
            pltpu.VMEM((copies, rows, step * width), BF16),
            pltpu.VMEM((groups * pad, width), F32),
            pltpu.VMEM(forward.shape, F32),
            pltpu.VMEM(mirror.shape, F32),
            pltpu.VMEM(one_way, BF16),
            pltpu.VMEM(one_way, BF16),
            pltpu.SemaphoreType.DMA,
            pltpu.SemaphoreType.DMA((copies,)),
            pltpu.SemaphoreType.DMA((2,)),
            pltpu.SemaphoreType.DMA((2,)),
        ],
        compiler_params=pltpu.CompilerParams(vmem_limit_bytes=60 * MIB),
        cost_estimate=pl.CostEstimate(
            flops=4 * rows * cols * groups * width,
            bytes_accessed=4 * groups * width * (rows + cols),
            transcendentals=0,
        ),
        name="contract_last",
    )(u2, u1, c, forward, mirror)


def per_device(cond_dens, val_dens, trial_vecs, eig_vals, block_pairs, slot_block):
    kpoints, nv_bands, columns = trial_vecs.shape
    nc_bands = cond_dens.shape[2]
    nvec = columns // nc_bands
    lanes = cond_dens.shape[3]
    cores, eigs = lax.axis_size("c"), lax.axis_size("x")
    chip = lax.axis_index("z") * lax.axis_size("y") + lax.axis_index("y")
    slot = chip * cores + lax.axis_index("c")
    kp = ("z", "y", "c")

    late = 128
    early = lanes - late
    sent_early = gather_rows(cond_dens, slot_block, 0, early, 8)
    owned_early = lax.all_to_all(sent_early, kp, split_axis=0, concat_axis=0, tiled=True)
    pair = block_pairs[slot_block[slot]]
    near = trial_vecs[pair[0]] * (pair[0] < pair[1]).astype(BF16)
    far = trial_vecs[pair[1]]
    near = near.reshape(nv_bands, columns).T
    far = far.reshape(nv_bands, columns).T
    eig = eig_vals[None, :]
    values = val_dens[0]
    u2_early, u2_late = expand(far, values, eig, (early, late), nvec, 4)
    u1_early, u1_late = expand(near, values.transpose(1, 0, 2), eig, (early, late), nvec, 4)

    sent_late = gather_rows(cond_dens, slot_block, early, late, 2)
    both = block_pairs[lax.dynamic_slice_in_dim(slot_block, chip * cores, cores)]
    hits = (jnp.arange(kpoints, dtype=jnp.int32) == both[:, :, None]).astype(F32)
    sent_late, owned_early, u2_early, u1_early, hits = lax.optimization_barrier(
        (sent_late, owned_early, u2_early, u1_early, hits)
    )
    owned_late = lax.all_to_all(sent_late, kp, split_axis=0, concat_axis=0, tiled=True)
    owned_early = owned_early.reshape(nc_bands, nc_bands, early)
    owned_late = owned_late.reshape(nc_bands, nc_bands, late)

    forward, mirror = contract_first(
        u2_early, owned_early.transpose(1, 0, 2), u1_early, owned_early, 8
    )
    part_rows = nc_bands // eigs
    half_lanes = nv_bands * nvec // cores
    pieces = (cores * eigs, 2, part_rows, half_lanes)
    sums = contract_last(u2_late, u1_late, owned_late, forward, mirror, pieces, 8, 6)

    arrived = lax.all_to_all(sums, ("c", "x"), split_axis=0, concat_axis=0, tiled=True)
    arrived = arrived.reshape(cores, eigs, 2, part_rows, half_lanes).astype(F32).sum(1)
    placed = jnp.zeros((kpoints, part_rows, half_lanes), F32)
    for core in range(cores):
        for which in range(2):
            placed = placed + hits[core, which][:, None, None] * arrived[core, which]
    image = lax.all_to_all(placed.astype(BF16), ("z", "y"), split_axis=0, concat_axis=0, tiled=True)
    image = image.astype(F32).sum(0).reshape(part_rows, nv_bands // cores, nvec)
    return image.transpose(1, 0, 2).reshape(nv_bands // cores, part_rows * nvec)


def solution(mesh):
    kp, eig = mesh.devices.shape
    fine = Mesh(mesh.devices.reshape(8, kp // 16, 2, eig), ("z", "y", "c", "x"))
    kp_axes = ("z", "y", "c")
    return jax.shard_map(
        per_device,
        mesh=fine,
        in_specs=(
            P(None, kp_axes, None, "x"),
            P(kp_axes, None, None, "x"),
            P(),
            P("x"),
            P(),
            P(),
        ),
        out_specs=P(kp_axes, "x"),
        check_vma=False,
    )
```
